32 devices in a mesh: imp: 4 (over x, core), dev: 8 (over z, y).
Axes of the slice: x: 2, y: 2, z: 4, core: 2. Of those that a mesh axis runs over, the one named last changes fastest.
Arguments:
- values: bfloat16 [2048, 256, 256], P(('imp', 'dev')), may hold values from 0 to 1
- costs: bfloat16 [2048, 256, 256], P(('imp', 'dev')), may hold values from 0.19921875 to 2
- block_ids: int32 [2048], P(('imp', 'dev')), may hold values from 0 to 31
- row_counts: int32 [2048], P(('imp', 'dev')), may hold values from 32 to 256
- adv_map: int32 [8192], P(('imp', 'dev')), may hold values from 0 to 2047
- camp_limits: float32 [8192], P(('imp', 'dev')), may hold values from 2048 to 16384
- adv_limits: float32 [2048], replicated, may hold values from 8192 to 32768
- camp_duals: float32 [8192], P(('imp', 'dev')), may hold values from 0 to 0.5
- adv_duals: float32 [2048], replicated, may hold values from 0 to 0.2
Outputs:
- camp_final: float32 [8192], P(('imp', 'dev'))
- adv_final: float32 [2048], replicated
- spend: float32 [8192], P(('imp', 'dev'))
The draws below stay inside these ranges and needn't reach their ends.
All inputs are finite; a program needn't handle non-finite values.
Results may differ from the reference program's by a relative error of at most 0.0003.
Values sent between devices are 32-bit elements; how exact they have to be, the bound alone decides.
A program may use at most 64 MiB of HBM per device.

```python
import math
import jax
import jax.numpy as jnp
from jax import lax

CW = 256
R = 256
NB = 64
CBD = 1
NADV = 2048
ITERS = 2
BLOCKS = 2048
NCB = 32
NCAMP = 8192
DEVICES = 32


def set_ends(entries, own_key, least, top_value):
    longest = entries.shape.index(max(entries.shape))
    spots = []
    for shift in (0, 1):
        where = [jax.random.randint(jax.random.fold_in(own_key, axis), (), 0, length) for axis, length in enumerate(entries.shape)]
        where[longest] = (where[longest] + shift) % entries.shape[longest]
        spots.append(tuple(where))
    return entries.at[spots[0]].set(least).at[spots[1]].set(top_value)


def block_scale(key, extent, cuts, smallest, high):
    gain = 1.0
    for dim, blocks in cuts:
        steps = jax.random.uniform(jax.random.fold_in(jax.random.fold_in(key, 6), dim), (blocks,), jnp.float32, smallest / len(cuts), high / len(cuts))
        gain = gain * jnp.repeat(jnp.exp(steps), extent[dim] // blocks).reshape((-1,) + (1,) * (len(extent) - 1 - dim))
    return gain


def setup_inputs(seed: int = 0) -> dict:
    key_list = jax.random.split(jax.random.key(seed), 10)
    return {
        "values": jnp.clip(1.0 * jax.random.uniform(key_list[0], (BLOCKS, R, CW), jnp.float32) ** block_scale(key_list[0], (BLOCKS, R, CW), ((0, 32),), -0.2, 0.2), 0.0, 1.0).astype(jnp.bfloat16),
        "costs": jnp.clip(jnp.exp(math.log(2.0) - 2.306499 * jax.random.uniform(key_list[1], (BLOCKS, R, CW), jnp.float32) ** block_scale(key_list[1], (BLOCKS, R, CW), ((0, 32),), -0.2, 0.2)), 0.19921875, 2.0).astype(jnp.bfloat16),
        "block_ids": set_ends(jax.random.randint(key_list[2], (BLOCKS,), 0, NCB), jax.random.fold_in(key_list[2], 1), 0, NCB - 1).astype(jnp.int32),
        "row_counts": set_ends(jax.random.randint(key_list[3], (BLOCKS,), R // 8, R + 1), jax.random.fold_in(key_list[3], 1), R // 8, R).astype(jnp.int32),
        "adv_map": set_ends(jax.random.randint(key_list[4], (NCAMP,), 0, NADV), jax.random.fold_in(key_list[4], 1), 0, NADV - 1).astype(jnp.int32),
        "camp_limits": jnp.clip(jnp.exp(math.log(16384.0) - 2.0794415 * jax.random.uniform(key_list[5], (NCAMP,), jnp.float32) ** block_scale(key_list[5], (NCAMP,), ((0, 32),), -0.2, 0.2)), 2048.0, 16384.0),
        "adv_limits": jnp.clip(jnp.exp(jax.random.uniform(key_list[6], (NADV,), jnp.float32, math.log(8192.0), math.log(32768.0))), 8192.0, 32768.0),
        "camp_duals": jnp.clip(0.5 * jax.random.uniform(key_list[7], (NCAMP,), jnp.float32) ** block_scale(key_list[7], (NCAMP,), ((0, 32),), -0.2, 0.2), 0.0, 0.5),
        "adv_duals": jnp.clip(jax.random.uniform(key_list[8], (NADV,), jnp.float32, 0.0, 0.2), 0.0, 0.2),
    }


def block_spend(values, costs, price_blocks, row_counts):
    rows = jnp.arange(values.shape[1], dtype=jnp.int32)
    live = (rows[None, :] < row_counts[:, None]).astype(jnp.float32)
    cost_f = costs.astype(jnp.float32)
    x_val = jnp.clip((values.astype(jnp.float32) - cost_f * price_blocks[:, None, :]) / 0.5, 0.0, 1.0)
    x_val = x_val * live[:, :, None]
    return jnp.sum(cost_f * x_val, axis=1)


def reference(values, costs, block_ids, row_counts, adv_map, camp_limits, adv_limits, camp_duals, adv_duals):
    lam = camp_duals
    mu = adv_duals
    eta = CBD / (4.0 * R * NB)
    eta_adv = NADV * CBD / (4.0 * R * NB * NCAMP)
    val_dev = values.reshape(DEVICES, NB, R, CW)
    cost_dev = costs.reshape(DEVICES, NB, R, CW)
    ids_dev = block_ids.reshape(DEVICES, NB)
    cnt_dev = row_counts.reshape(DEVICES, NB)
    spend = jnp.zeros((NCAMP,), jnp.float32)
    for step in range(ITERS):
        price = (lam + mu[adv_map]).reshape(NCB, CW)

        def one_device(args):
            vals, csts, ids, cnts = args
            return block_spend(vals, csts, price[ids], cnts)

        contrib = lax.map(one_device, (val_dev, cost_dev, ids_dev, cnt_dev)).reshape(BLOCKS, CW)
        spend = jax.ops.segment_sum(contrib, block_ids, NCB).reshape(NCAMP)
        adv_spend = jax.ops.segment_sum(spend, adv_map, NADV)
        lam = jnp.maximum(0.0, lam + eta * (spend - camp_limits))
        mu = jnp.maximum(0.0, mu + eta_adv * (adv_spend - adv_limits))
    return lam, mu, spend
```

```python
import functools

import jax
import jax.numpy as jnp
from jax import lax
from jax.experimental import pallas as pl
from jax.experimental.pallas import tpu as pltpu
from jax.sharding import PartitionSpec as P

ITERS = 2
LANES = 128
SLAB = 16
SUBLANES = 8
CHUNKS = 8
MESH = pl.DeviceIdType.MESH


def split3(x):
    one = x.astype(jnp.bfloat16)
    rest = x - one.astype(jnp.float32)
    two = rest.astype(jnp.bfloat16)
    three = (rest - two.astype(jnp.float32)).astype(jnp.bfloat16)
    return jnp.concatenate([one, two, three], axis=0)


def sum3(x):
    m = x.shape[0] // 3
    return x[:m] + x[m : 2 * m] + x[2 * m :]


def low_onehot(adv):
    width = adv.shape[1]
    rows = lax.broadcasted_iota(jnp.int32, (LANES, width), 0)
    hit = rows == jnp.bitwise_and(adv, LANES - 1)
    return jnp.where(hit, 1.0, 0.0).astype(jnp.bfloat16)


def high_onehot(adv, groups):
    width = adv.shape[1]
    rows = lax.broadcasted_iota(jnp.int32, (groups, width), 0)
    return jnp.where(rows == lax.shift_right_logical(adv, 7), 1.0, 0.0)


def take(mu3, low, high):
    picked = jnp.dot(mu3, low, preferred_element_type=jnp.float32)
    return jnp.sum(sum3(picked) * high, axis=0, keepdims=True)


def kernel(
    n,
    n_dev,
    eta,
    eta_adv,
    counts_s,
    values,
    costs,
    ids_v,
    adv_ref,
    lim_ref,
    adv_lim_ref,
    lam_ref,
    mu_ref,
    lam_out,
    mu_out,
    spend_out,
    vbuf,
    cbuf,
    price,
    static,
    low,
    high,
    cap,
    contrib,
    asked,
    part,
    got,
    allspend,
    load_sem,
    send_sem,
    recv_sem,
):
    blocks, rows, width = vbuf.shape
    groups = mu_ref.shape[0]
    me = lax.axis_index("imp") * n_dev + lax.axis_index("dev")
    step_blocks = blocks // CHUNKS

    def load(i):
        where = pl.ds(i * step_blocks, step_blocks)
        return (
            pltpu.make_async_copy(values.at[where], vbuf.at[where], load_sem.at[0, i]),
            pltpu.make_async_copy(costs.at[where], cbuf.at[where], load_sem.at[1, i]),
        )

    for i in range(CHUNKS):
        for copy in load(i):
            copy.start()

    barrier = pltpu.get_barrier_semaphore()

    def peer(d):
        return lax.rem(me + d, n)

    def place(k):
        return (k // n_dev, lax.rem(k, n_dev))

    @pl.loop(1, n)
    def _(d):
        pl.semaphore_signal(barrier, inc=1, device_id=place(peer(d)), device_id_type=MESH)

    def lanes(k):
        return pl.ds(pl.multiple_of(k * width, width), width)

    def share(ref, phase):
        @pl.loop(1, n)
        def _(d):
            spot = ref.at[:, lanes(me)]
            pltpu.make_async_remote_copy(
                src_ref=spot,
                dst_ref=spot,
                send_sem=send_sem.at[phase],
                recv_sem=recv_sem.at[phase],
                device_id=place(peer(d)),
                device_id_type=MESH,
            ).start()

    def wait_all(ref, sem):
        span = ref.at[:, pl.ds(0, (n - 1) * width)]
        pltpu.make_async_copy(span, span, sem).wait()

    def scatter(phase):
        @pl.loop(1, n)
        def _(d):
            to = peer(d)
            pltpu.make_async_remote_copy(
                src_ref=part.at[to],
                dst_ref=got.at[phase, d - 1],
                send_sem=send_sem.at[2 + phase],
                recv_sem=recv_sem.at[2 + phase],
                device_id=place(to),
                device_id_type=MESH,
            ).start()

    def wait_scatter(sem, phase):
        span = got.at[phase]
        pltpu.make_async_copy(span, span, sem).wait()

    adv = adv_ref[...]
    lam = lam_ref[...]
    mu = mu_ref[...]
    price[0, :, lanes(me)] = lam + take(split3(mu), low_onehot(adv), high_onehot(adv, groups))
    static[:, lanes(me)] = jnp.concatenate(
        [lam, adv.astype(jnp.float32), lim_ref[...], jnp.zeros_like(lam)], axis=0
    )
    live_rows = lax.broadcasted_iota(jnp.int32, (SLAB, LANES), 0)
    for k in range(SLAB + 1):
        cap[k] = jnp.where(live_rows < k, 0.5, 0.0)

    pl.semaphore_wait(barrier, n - 1)
    share(price.at[0], 0)
    share(static, 1)
    wait_all(price.at[0], recv_sem.at[0])

    campaign = lax.broadcasted_iota(jnp.int32, (part.shape[0], blocks), 0)
    owner = jnp.where(campaign == ids_v[...], 1.0, 0.0).astype(jnp.bfloat16)
    asks3 = jnp.concatenate([owner, owner, owner], axis=0)
    wide = lax.broadcasted_iota(jnp.int32, (blocks, blocks * SUBLANES), 1)
    from_block = lax.broadcasted_iota(jnp.int32, (blocks, blocks * SUBLANES), 0)
    spread = jnp.where(lax.shift_right_logical(wide, 3) == from_block, 1.0, 0.0)
    owner = jnp.dot(
        owner, spread.astype(jnp.bfloat16), preferred_element_type=jnp.float32
    ).astype(jnp.bfloat16)
    owner3 = jnp.concatenate([owner, owner, owner], axis=1)

    def block_pass(b, it):
        prices = [
            jnp.broadcast_to(asked[b, :, h : h + LANES], (SLAB, LANES))
            for h in range(0, width, LANES)
        ]
        totals = [jnp.zeros((SLAB, LANES), jnp.float32) for _ in prices]
        count = counts_s[b]
        for s in range(0, rows, SLAB):
            top = cap[jnp.minimum(jnp.maximum(count - s, 0), SLAB)]
            for h, p in enumerate(prices):
                at = pl.ds(h * LANES, LANES)
                v = vbuf[b, pl.ds(s, SLAB), at].astype(jnp.float32)
                c = cbuf[b, pl.ds(s, SLAB), at].astype(jnp.float32)
                x = jnp.minimum(jnp.maximum(v - c * p, 0.0), top)
                totals[h] = totals[h] + c * x
        for h, total in enumerate(totals):
            where = pl.ds(pl.multiple_of(b * SUBLANES, SUBLANES), SUBLANES)
            contrib[where, pl.ds(h * LANES, LANES)] = 2.0 * (
                total[:SUBLANES] + total[SUBLANES:]
            )

    for it in range(ITERS):
        offers = jnp.concatenate(
            [price[it, :, pl.ds(k * width, width)] for k in range(part.shape[0])], axis=0
        )
        asking = lax.dot_general(
            asks3, split3(offers), (((0,), (0,)), ((), ())), preferred_element_type=jnp.float32
        )
        for b in range(blocks):
            asked[b] = asking[b : b + 1]
        for i in range(CHUNKS if it == 0 else 1):
            if it == 0:
                for copy in load(i):
                    copy.wait()
            span = step_blocks if it == 0 else blocks

            @pl.loop(i * span, (i + 1) * span)
            def _(b):
                block_pass(b, it)

        mine = jnp.dot(owner3, split3(contrib[...]), preferred_element_type=jnp.float32)
        if it > 0:
            wait_scatter(send_sem.at[2 + it - 1], it - 1)
        for k in range(part.shape[0]):
            part[k] = mine[k : k + 1]
        scatter(it)
        if it == 0:
            wait_all(static, recv_sem.at[1])
            for k in range(n):
                every = static[1:2, pl.ds(k * width, width)].astype(jnp.int32)
                low[:, pl.ds(k * width, width)] = low_onehot(every)
                high[:, pl.ds(k * width, width)] = high_onehot(every, groups)
        wait_scatter(recv_sem.at[2 + it], it)
        spend = part[me] + jnp.sum(got[it], axis=0)
        allspend[it, :, lanes(me)] = spend
        share(allspend.at[it], 4 + it)
        lam = jnp.maximum(0.0, lam + eta * (spend - lim_ref[...]))
        wait_all(allspend.at[it], recv_sem.at[4 + it])

        adv_spend = jnp.zeros((3 * groups, LANES), jnp.float32)
        stretch = min(n, 32) * width
        for first in range(0, n * width, stretch):
            at = pl.ds(first, stretch)
            adv_spend = adv_spend + lax.dot_general(
                split3(high[:, at] * allspend[it, :, at]),
                low[:, at],
                (((1,), (1,)), ((), ())),
                preferred_element_type=jnp.float32,
            )
        mu = jnp.maximum(0.0, mu + eta_adv * (sum3(adv_spend) - adv_lim_ref[...]))
        if it < ITERS - 1:
            mu3 = split3(mu)
            for first in range(0, n * width, stretch):
                at = pl.ds(first, stretch)
                lam_all = jnp.maximum(
                    0.0, static[0:1, at] + eta * (allspend[it, :, at] - static[2:3, at])
                )
                price[it + 1, :, at] = lam_all + take(mu3, low[:, at], high[:, at])
    lam_out[...] = lam
    mu_out[...] = mu
    spend_out[...] = spend
    wait_all(price.at[0], send_sem.at[0])
    wait_all(static, send_sem.at[1])
    wait_scatter(send_sem.at[2 + ITERS - 1], ITERS - 1)
    for it in range(ITERS):
        wait_all(allspend.at[it], send_sem.at[4 + it])


def body(
    n,
    n_dev,
    values,
    costs,
    block_ids,
    row_counts,
    adv_map,
    camp_limits,
    adv_limits,
    camp_duals,
    adv_duals,
):
    blocks, rows, width = values.shape
    owned = camp_duals.shape[0]
    total = owned * n
    num_adv = adv_duals.shape[0]
    groups = num_adv // LANES
    eta = owned // width / (4.0 * rows * blocks)
    eta_adv = num_adv * (owned // width) / (4.0 * rows * blocks * total)
    smem = pl.BlockSpec(memory_space=pltpu.SMEM)
    vmem = pl.BlockSpec(memory_space=pltpu.VMEM)
    hbm = pl.BlockSpec(memory_space=pl.ANY)
    lam, mu, spend = pl.pallas_call(
        functools.partial(kernel, n, n_dev, eta, eta_adv),
        out_shape=(
            jax.ShapeDtypeStruct((1, owned), jnp.float32),
            jax.ShapeDtypeStruct((groups, LANES), jnp.float32),
            jax.ShapeDtypeStruct((1, owned), jnp.float32),
        ),
        in_specs=[smem, hbm, hbm] + [vmem] * 6,
        out_specs=(vmem, vmem, vmem),
        scratch_shapes=[
            pltpu.VMEM((blocks, rows, width), jnp.bfloat16),
            pltpu.VMEM((blocks, rows, width), jnp.bfloat16),
            pltpu.VMEM((ITERS, 1, total), jnp.float32),
            pltpu.VMEM((4, total), jnp.float32),
            pltpu.VMEM((LANES, total), jnp.bfloat16),
            pltpu.VMEM((groups, total), jnp.float32),
            pltpu.VMEM((SLAB + 1, SLAB, LANES), jnp.float32),
            pltpu.VMEM((blocks * SUBLANES, width), jnp.float32),
            pltpu.VMEM((blocks, 1, width), jnp.float32),
            pltpu.VMEM((total // width, 1, width), jnp.float32),
            pltpu.VMEM((ITERS, n - 1, 1, width), jnp.float32),
            pltpu.VMEM((ITERS, 1, total), jnp.float32),
            pltpu.SemaphoreType.DMA((2, CHUNKS)),
            pltpu.SemaphoreType.DMA((6,)),
            pltpu.SemaphoreType.DMA((6,)),
        ],
        compiler_params=pltpu.CompilerParams(
            collective_id=0, has_side_effects=True, vmem_limit_bytes=56 * 1024 * 1024
        ),
        cost_estimate=pl.CostEstimate(
            flops=ITERS * 8 * blocks * rows * width,
            bytes_accessed=4 * blocks * rows * width,
            transcendentals=0,
        ),
    )(
        row_counts,
        values,
        costs,
        block_ids.reshape(1, blocks),
        adv_map.reshape(1, owned),
        camp_limits.reshape(1, owned),
        adv_limits.reshape(groups, LANES),
        camp_duals.reshape(1, owned),
        adv_duals.reshape(groups, LANES),
    )
    return lam.reshape(owned), mu.reshape(num_adv), spend.reshape(owned)


def solution(mesh):
    both = P(("imp", "dev"))
    blocked = P(("imp", "dev"), None, None)
    return jax.shard_map(
        functools.partial(body, mesh.size, mesh.shape["dev"]),
        mesh=mesh,
        in_specs=(blocked, blocked, both, both, both, both, P(), both, P()),
        out_specs=(both, P(), both),
        check_vma=False,
    )
```

```python
import functools

import jax
import jax.numpy as jnp
from jax import lax
from jax.experimental import pallas as pl
from jax.experimental.pallas import tpu as pltpu
from jax.sharding import PartitionSpec as P

ITERS = 2
LANES = 128
SLAB = 16
SUBLANES = 8
CHUNKS = 8
MESH = pl.DeviceIdType.MESH


def split3(x):
    one = x.astype(jnp.bfloat16)
    rest = x - one.astype(jnp.float32)
    two = rest.astype(jnp.bfloat16)
    three = (rest - two.astype(jnp.float32)).astype(jnp.bfloat16)
    return jnp.concatenate([one, two, three], axis=0)


def split2(x):
    one = x.astype(jnp.bfloat16)
    return jnp.concatenate([one, (x - one.astype(jnp.float32)).astype(jnp.bfloat16)], axis=0)


def sum3(x):
    m = x.shape[0] // 3
    return x[:m] + x[m : 2 * m] + x[2 * m :]


def low_onehot(adv):
    width = adv.shape[1]
    rows = lax.broadcasted_iota(jnp.int32, (LANES, width), 0)
    hit = rows == jnp.bitwise_and(adv, LANES - 1)
    return jnp.where(hit, 1.0, 0.0).astype(jnp.bfloat16)


def high_onehot(adv, groups):
    width = adv.shape[1]
    rows = lax.broadcasted_iota(jnp.int32, (groups, width), 0)
    return jnp.where(rows == lax.shift_right_logical(adv, 7), 1.0, 0.0)


def take(mu3, low, high):
    picked = jnp.dot(mu3, low, preferred_element_type=jnp.float32)
    return jnp.sum(sum3(picked) * high, axis=0, keepdims=True)


def kernel(
    n,
    n_dev,
    eta,
    eta_adv,
    ids_s,
    counts_s,
    values,
    costs,
    ids_v,
    adv_ref,
    lim_ref,
    adv_lim_ref,
    lam_ref,
    mu_ref,
    result,
    vbuf,
    cbuf,
    price,
    static,
    low,
    high,
    cap,
    contrib,
    part,
    got,
    allspend,
    load_sem,
    send_sem,
    recv_sem,
):
    blocks, rows, width = vbuf.shape
    groups = mu_ref.shape[0]
    me = lax.axis_index("imp") * n_dev + lax.axis_index("dev")
    step_blocks = blocks // CHUNKS

    def load(i):
        where = pl.ds(i * step_blocks, step_blocks)
        return (
            pltpu.make_async_copy(values.at[where], vbuf.at[where], load_sem.at[0, i]),
            pltpu.make_async_copy(costs.at[where], cbuf.at[where], load_sem.at[1, i]),
        )

    for i in range(CHUNKS):
        for copy in load(i):
            copy.start()

    barrier = pltpu.get_barrier_semaphore()

    def peer(d):
        return lax.rem(me + d, n)

    def place(k):
        return (k // n_dev, lax.rem(k, n_dev))

    @pl.loop(1, n)
    def _(d):
        pl.semaphore_signal(barrier, inc=1, device_id=place(peer(d)), device_id_type=MESH)

    def lanes(k):
        return pl.ds(pl.multiple_of(k * width, width), width)

    def share(ref, phase):
        spot = ref.at[me] if len(ref.shape) == 3 else ref.at[:, lanes(me)]

        @pl.loop(1, n)
        def _(d):
            pltpu.make_async_remote_copy(
                src_ref=spot,
                dst_ref=spot,
                send_sem=send_sem.at[phase],
                recv_sem=recv_sem.at[phase],
                device_id=place(peer(d)),
                device_id_type=MESH,
            ).start()

    def wait_all(ref, sem):
        if len(ref.shape) == 3:
            span = ref.at[pl.ds(0, n - 1)]
        else:
            span = ref.at[:, pl.ds(0, (n - 1) * width)]
        pltpu.make_async_copy(span, span, sem).wait()

    def scatter(phase):
        @pl.loop(1, n)
        def _(d):
            to = peer(d)
            pltpu.make_async_remote_copy(
                src_ref=part.at[to],
                dst_ref=got.at[phase, d - 1],
                send_sem=send_sem.at[2 + phase],
                recv_sem=recv_sem.at[2 + phase],
                device_id=place(to),
                device_id_type=MESH,
            ).start()

    def wait_scatter(sem, phase):
        span = got.at[phase]
        pltpu.make_async_copy(span, span, sem).wait()

    adv = adv_ref[...]
    lam = lam_ref[...]
    mu = mu_ref[...]
    price[0, me] = lam + take(split3(mu), low_onehot(adv), high_onehot(adv, groups))
    static[:, lanes(me)] = jnp.concatenate(
        [lam, adv.astype(jnp.float32), lim_ref[...], jnp.zeros_like(lam)], axis=0
    )
    live_rows = lax.broadcasted_iota(jnp.int32, (SLAB, LANES), 0)
    for k in range(SLAB + 1):
        cap[k] = jnp.where(live_rows < k, 0.5, 0.0)

    pl.semaphore_wait(barrier, n - 1)
    share(price.at[0], 0)
    share(static, 1)
    wait_all(price.at[0], recv_sem.at[0])

    campaign = lax.broadcasted_iota(jnp.int32, (part.shape[0], blocks), 0)
    owner = jnp.where(campaign == ids_v[...], 1.0, 0.0).astype(jnp.bfloat16)
    wide = lax.broadcasted_iota(jnp.int32, (blocks, blocks * SUBLANES), 1)
    from_block = lax.broadcasted_iota(jnp.int32, (blocks, blocks * SUBLANES), 0)
    spread = jnp.where(lax.shift_right_logical(wide, 3) == from_block, 1.0, 0.0)
    owner = jnp.dot(
        owner, spread.astype(jnp.bfloat16), preferred_element_type=jnp.float32
    ).astype(jnp.bfloat16)
    owner2 = jnp.concatenate([owner, owner], axis=1)

    def block_pass(b, it):
        row = price[it, ids_s[b]]
        prices = [
            jnp.broadcast_to(row[:, h : h + LANES], (SLAB, LANES))
            for h in range(0, width, LANES)
        ]
        totals = [jnp.zeros((SLAB, LANES), jnp.float32) for _ in prices]
        count = counts_s[b]
        for s in range(0, rows, SLAB):
            top = cap[jnp.minimum(jnp.maximum(count - s, 0), SLAB)]
            for h, p in enumerate(prices):
                at = pl.ds(h * LANES, LANES)
                v = vbuf[b, pl.ds(s, SLAB), at].astype(jnp.float32)
                c = cbuf[b, pl.ds(s, SLAB), at].astype(jnp.float32)
                x = jnp.minimum(jnp.maximum(v - c * p, 0.0), top)
                totals[h] = totals[h] + c * x
        for h, total in enumerate(totals):
            where = pl.ds(pl.multiple_of(b * SUBLANES, SUBLANES), SUBLANES)
            contrib[where, pl.ds(h * LANES, LANES)] = 2.0 * (
                total[:SUBLANES] + total[SUBLANES:]
            )

    for it in range(ITERS):
        for i in range(CHUNKS if it == 0 else 1):
            if it == 0:
                for copy in load(i):
                    copy.wait()
            span = step_blocks if it == 0 else blocks

            @pl.loop(i * span, (i + 1) * span)
            def _(b):
                block_pass(b, it)

        mine = jnp.dot(owner2, split2(contrib[...]), preferred_element_type=jnp.float32)
        if it > 0:
            wait_scatter(send_sem.at[2 + it - 1], it - 1)
        for k in range(part.shape[0]):
            part[k] = mine[k : k + 1]
        scatter(it)
        if it == 0:
            wait_all(static, recv_sem.at[1])
            for k in range(n):
                every = static[1:2, pl.ds(k * width, width)].astype(jnp.int32)
                low[:, pl.ds(k * width, width)] = low_onehot(every)
                high[:, pl.ds(k * width, width)] = high_onehot(every, groups)
        wait_scatter(recv_sem.at[2 + it], it)
        spend = part[me] + jnp.sum(got[it], axis=0)
        allspend[it, :, lanes(me)] = spend
        share(allspend.at[it], 4 + it)
        lam = jnp.maximum(0.0, lam + eta * (spend - lim_ref[...]))
        wait_all(allspend.at[it], recv_sem.at[4 + it])

        adv_spend = jnp.zeros((3 * groups, LANES), jnp.float32)
        stretch = min(n, 32) * width
        for first in range(0, n * width, stretch):
            at = pl.ds(first, stretch)
            adv_spend = adv_spend + lax.dot_general(
                split3(high[:, at] * allspend[it, :, at]),
                low[:, at],
                (((1,), (1,)), ((), ())),
                preferred_element_type=jnp.float32,
            )
        mu = jnp.maximum(0.0, mu + eta_adv * (sum3(adv_spend) - adv_lim_ref[...]))
        if it < ITERS - 1:
            mu3 = split3(mu)
            for first in range(0, n * width, stretch):
                at = pl.ds(first, stretch)
                lam_all = jnp.maximum(
                    0.0, static[0:1, at] + eta * (allspend[it, :, at] - static[2:3, at])
                )
                new = lam_all + take(mu3, low[:, at], high[:, at])
                for k in range(stretch // width):
                    price[it + 1, first // width + k] = new[:, k * width : (k + 1) * width]
    tiles = width // LANES
    for k in range(tiles):
        at = slice(k * LANES, (k + 1) * LANES)
        result[k : k + 1] = lam[:, at]
        result[tiles + k : tiles + k + 1] = spend[:, at]
    result[SUBLANES:] = mu
    wait_all(price.at[0], send_sem.at[0])
    wait_all(static, send_sem.at[1])
    wait_scatter(send_sem.at[2 + ITERS - 1], ITERS - 1)
    for it in range(ITERS):
        wait_all(allspend.at[it], send_sem.at[4 + it])


def deal(result, lam_out, mu_out, spend_out):
    tiles = lam_out.shape[1] // LANES
    for k in range(tiles):
        at = slice(k * LANES, (k + 1) * LANES)
        lam_out[:, at] = result[k : k + 1]
        spend_out[:, at] = result[tiles + k : tiles + k + 1]
    mu_out[...] = result[SUBLANES:]


def body(
    n,
    n_dev,
    values,
    costs,
    block_ids,
    row_counts,
    adv_map,
    camp_limits,
    adv_limits,
    camp_duals,
    adv_duals,
):
    blocks, rows, width = values.shape
    owned = camp_duals.shape[0]
    total = owned * n
    num_adv = adv_duals.shape[0]
    groups = num_adv // LANES
    eta = owned // width / (4.0 * rows * blocks)
    eta_adv = num_adv * (owned // width) / (4.0 * rows * blocks * total)
    smem = pl.BlockSpec(memory_space=pltpu.SMEM)
    vmem = pl.BlockSpec(memory_space=pltpu.VMEM)
    hbm = pl.BlockSpec(memory_space=pl.ANY)
    result = pl.pallas_call(
        functools.partial(kernel, n, n_dev, eta, eta_adv),
        out_shape=jax.ShapeDtypeStruct((SUBLANES + groups, LANES), jnp.float32),
        in_specs=[smem, smem, hbm, hbm] + [vmem] * 6,
        out_specs=vmem,
        scratch_shapes=[
            pltpu.VMEM((blocks, rows, width), jnp.bfloat16),
            pltpu.VMEM((blocks, rows, width), jnp.bfloat16),
            pltpu.VMEM((ITERS, n, 1, width), jnp.float32),
            pltpu.VMEM((4, total), jnp.float32),
            pltpu.VMEM((LANES, total), jnp.bfloat16),
            pltpu.VMEM((groups, total), jnp.float32),
            pltpu.VMEM((SLAB + 1, SLAB, LANES), jnp.float32),
            pltpu.VMEM((blocks * SUBLANES, width), jnp.float32),
            pltpu.VMEM((total // width, 1, width), jnp.float32),
            pltpu.VMEM((ITERS, n - 1, 1, width), jnp.float32),
            pltpu.VMEM((ITERS, 1, total), jnp.float32),
            pltpu.SemaphoreType.DMA((2, CHUNKS)),
            pltpu.SemaphoreType.DMA((6,)),
            pltpu.SemaphoreType.DMA((6,)),
        ],
        compiler_params=pltpu.CompilerParams(
            collective_id=0, has_side_effects=True, vmem_limit_bytes=56 * 1024 * 1024
        ),
        cost_estimate=pl.CostEstimate(
            flops=ITERS * 8 * blocks * rows * width,
            bytes_accessed=4 * blocks * rows * width,
            transcendentals=0,
        ),
    )(
        block_ids,
        row_counts,
        values,
        costs,
        block_ids.reshape(1, blocks),
        adv_map.reshape(1, owned),
        camp_limits.reshape(1, owned),
        adv_limits.reshape(groups, LANES),
        camp_duals.reshape(1, owned),
        adv_duals.reshape(groups, LANES),
    )
    lam, mu, spend = pl.pallas_call(
        deal,
        out_shape=(
            jax.ShapeDtypeStruct((1, owned), jnp.float32),
            jax.ShapeDtypeStruct((groups, LANES), jnp.float32),
            jax.ShapeDtypeStruct((1, owned), jnp.float32),
        ),
        in_specs=[vmem],
        out_specs=(vmem, vmem, vmem),
    )(result)
    return lam.reshape(owned), mu.reshape(num_adv), spend.reshape(owned)


def solution(mesh):
    both = P(("imp", "dev"))
    blocked = P(("imp", "dev"), None, None)
    return jax.shard_map(
        functools.partial(body, mesh.size, mesh.shape["dev"]),
        mesh=mesh,
        in_specs=(blocked, blocked, both, both, both, both, P(), both, P()),
        out_specs=(both, P(), both),
        check_vma=False,
    )
```

```python
import functools

import jax
import jax.numpy as jnp
from jax import lax
from jax.experimental import pallas as pl
from jax.experimental.pallas import tpu as pltpu
from jax.sharding import PartitionSpec as P

ITERS = 2
LANES = 128
SLAB = 16
SUBLANES = 8
CHUNKS = 4
MESH = pl.DeviceIdType.MESH


def split3(x):
    one = x.astype(jnp.bfloat16)
    rest = x - one.astype(jnp.float32)
    two = rest.astype(jnp.bfloat16)
    three = (rest - two.astype(jnp.float32)).astype(jnp.bfloat16)
    return jnp.concatenate([one, two, three], axis=0)


def split2(x):
    one = x.astype(jnp.bfloat16)
    return jnp.concatenate([one, (x - one.astype(jnp.float32)).astype(jnp.bfloat16)], axis=0)


def sum3(x):
    m = x.shape[0] // 3
    return x[:m] + x[m : 2 * m] + x[2 * m :]


def low_onehot(adv):
    width = adv.shape[1]
    rows = lax.broadcasted_iota(jnp.int32, (LANES, width), 0)
    hit = rows == jnp.bitwise_and(adv, LANES - 1)
    return jnp.where(hit, 1.0, 0.0).astype(jnp.bfloat16)


def high_onehot(adv, groups):
    width = adv.shape[1]
    rows = lax.broadcasted_iota(jnp.int32, (groups, width), 0)
    return jnp.where(rows == lax.shift_right_logical(adv, 7), 1.0, 0.0)


def take(mu3, low, high):
    picked = jnp.dot(mu3, low, preferred_element_type=jnp.float32)
    return jnp.sum(sum3(picked) * high, axis=0, keepdims=True)


def kernel(
    n,
    n_dev,
    eta,
    eta_adv,
    ids_s,
    counts_s,
    values,
    costs,
    ids_v,
    adv_ref,
    lim_ref,
    adv_lim_ref,
    lam_ref,
    mu_ref,
    result,
    vbuf,
    cbuf,
    price,
    static,
    low,
    high,
    cap,
    contrib,
    part,
    got,
    allspend,
    load_sem,
    send_sem,
    recv_sem,
):
    blocks, rows, width = vbuf.shape
    groups = mu_ref.shape[0]
    me = lax.axis_index("imp") * n_dev + lax.axis_index("dev")
    step_blocks = blocks // CHUNKS

    def load(i):
        where = pl.ds(i * step_blocks, step_blocks)
        return (
            pltpu.make_async_copy(values.at[where], vbuf.at[where], load_sem.at[0, i]),
            pltpu.make_async_copy(costs.at[where], cbuf.at[where], load_sem.at[1, i]),
        )

    for i in range(CHUNKS):
        for copy in load(i):
            copy.start()

    barrier = pltpu.get_barrier_semaphore()

    def peer(d):
        return lax.rem(me + d, n)

    def place(k):
        return (k // n_dev, lax.rem(k, n_dev))

    @pl.loop(1, n, unroll=True)
    def _(d):
        pl.semaphore_signal(barrier, inc=1, device_id=place(peer(d)), device_id_type=MESH)

    def lanes(k):
        return pl.ds(pl.multiple_of(k * width, width), width)

    def share(ref, phase):
        spot = ref.at[me] if len(ref.shape) == 3 else ref.at[:, lanes(me)]

        @pl.loop(1, n, unroll=True)
        def _(d):
            pltpu.make_async_remote_copy(
                src_ref=spot,
                dst_ref=spot,
                send_sem=send_sem.at[phase],
                recv_sem=recv_sem.at[phase],
                device_id=place(peer(d)),
                device_id_type=MESH,
            ).start()

    def wait_all(ref, sem):
        if len(ref.shape) == 3:
            span = ref.at[pl.ds(0, n - 1)]
        else:
            span = ref.at[:, pl.ds(0, (n - 1) * width)]
        pltpu.make_async_copy(span, span, sem).wait()

    def scatter(phase):
        @pl.loop(1, n, unroll=True)
        def _(d):
            to = peer(d)
            pltpu.make_async_remote_copy(
                src_ref=part.at[to],
                dst_ref=got.at[phase, d - 1],
                send_sem=send_sem.at[2 + phase],
                recv_sem=recv_sem.at[2 + phase],
                device_id=place(to),
                device_id_type=MESH,
            ).start()

    def wait_scatter(sem, phase):
        span = got.at[phase]
        pltpu.make_async_copy(span, span, sem).wait()

    adv = adv_ref[...]
    lam = lam_ref[...]
    mu = mu_ref[...]
    price[0, me] = lam + take(split3(mu), low_onehot(adv), high_onehot(adv, groups))
    static[:, lanes(me)] = jnp.concatenate(
        [lam, adv.astype(jnp.float32), lim_ref[...], jnp.zeros_like(lam)], axis=0
    )
    live_rows = lax.broadcasted_iota(jnp.int32, (SLAB, LANES), 0)
    for k in range(SLAB + 1):
        cap[k] = jnp.where(live_rows < k, 0.5, 0.0)

    pl.semaphore_wait(barrier, n - 1)
    share(price.at[0], 0)
    share(static, 1)
    wait_all(price.at[0], recv_sem.at[0])

    campaign = lax.broadcasted_iota(jnp.int32, (part.shape[0], blocks), 0)
    owner = jnp.where(campaign == ids_v[...], 1.0, 0.0).astype(jnp.bfloat16)
    wide = lax.broadcasted_iota(jnp.int32, (blocks, blocks * SUBLANES), 1)
    from_block = lax.broadcasted_iota(jnp.int32, (blocks, blocks * SUBLANES), 0)
    spread = jnp.where(lax.shift_right_logical(wide, 3) == from_block, 1.0, 0.0)
    owner = jnp.dot(
        owner, spread.astype(jnp.bfloat16), preferred_element_type=jnp.float32
    ).astype(jnp.bfloat16)
    owner2 = jnp.concatenate([owner, owner], axis=1)

    def block_pass(b, it):
        row = price[it, ids_s[b]]
        prices = [
            jnp.broadcast_to(row[:, h : h + LANES], (SLAB, LANES))
            for h in range(0, width, LANES)
        ]
        totals = [jnp.zeros((SLAB, LANES), jnp.float32) for _ in prices]
        count = counts_s[b]
        for s in range(0, rows, SLAB):
            top = cap[jnp.minimum(jnp.maximum(count - s, 0), SLAB)]
            for h, p in enumerate(prices):
                at = pl.ds(h * LANES, LANES)
                v = vbuf[b, pl.ds(s, SLAB), at].astype(jnp.float32)
                c = cbuf[b, pl.ds(s, SLAB), at].astype(jnp.float32)
                x = jnp.minimum(jnp.maximum(v - c * p, 0.0), top)
                totals[h] = totals[h] + c * x
        for h, total in enumerate(totals):
            where = pl.ds(pl.multiple_of(b * SUBLANES, SUBLANES), SUBLANES)
            contrib[where, pl.ds(h * LANES, LANES)] = 2.0 * (
                total[:SUBLANES] + total[SUBLANES:]
            )

    for it in range(ITERS):
        for i in range(CHUNKS if it == 0 else 1):
            if it == 0:
                for copy in load(i):
                    copy.wait()
            span = step_blocks if it == 0 else blocks

            @pl.loop(i * span, (i + 1) * span, unroll=2)
            def _(b):
                block_pass(b, it)

        mine = jnp.dot(owner2, split2(contrib[...]), preferred_element_type=jnp.float32)
        if it > 0:
            wait_scatter(send_sem.at[2 + it - 1], it - 1)
        for k in range(part.shape[0]):
            part[k] = mine[k : k + 1]
        scatter(it)
        if it == 0:
            wait_all(static, recv_sem.at[1])
            for k in range(n):
                every = static[1:2, pl.ds(k * width, width)].astype(jnp.int32)
                low[:, pl.ds(k * width, width)] = low_onehot(every)
                high[:, pl.ds(k * width, width)] = high_onehot(every, groups)
        wait_scatter(recv_sem.at[2 + it], it)
        spend = part[me] + jnp.sum(got[it], axis=0)
        allspend[it, :, lanes(me)] = spend
        share(allspend.at[it], 4 + it)
        lam = jnp.maximum(0.0, lam + eta * (spend - lim_ref[...]))
        wait_all(allspend.at[it], recv_sem.at[4 + it])

        adv_spend = jnp.zeros((3 * groups, LANES), jnp.float32)
        stretch = min(n, 32) * width
        for first in range(0, n * width, stretch):
            at = pl.ds(first, stretch)
            adv_spend = adv_spend + lax.dot_general(
                split3(high[:, at] * allspend[it, :, at]),
                low[:, at],
                (((1,), (1,)), ((), ())),
                preferred_element_type=jnp.float32,
            )
        mu = jnp.maximum(0.0, mu + eta_adv * (sum3(adv_spend) - adv_lim_ref[...]))
        if it < ITERS - 1:
            mu3 = split3(mu)
            for first in range(0, n * width, stretch):
                at = pl.ds(first, stretch)
                lam_all = jnp.maximum(
                    0.0, static[0:1, at] + eta * (allspend[it, :, at] - static[2:3, at])
                )
                new = lam_all + take(mu3, low[:, at], high[:, at])
                for k in range(stretch // width):
                    price[it + 1, first // width + k] = new[:, k * width : (k + 1) * width]
    tiles = width // LANES
    for k in range(tiles):
        at = slice(k * LANES, (k + 1) * LANES)
        result[k : k + 1] = lam[:, at]
        result[tiles + k : tiles + k + 1] = spend[:, at]
    result[SUBLANES:] = mu
    wait_all(price.at[0], send_sem.at[0])
    wait_all(static, send_sem.at[1])
    wait_scatter(send_sem.at[2 + ITERS - 1], ITERS - 1)
    for it in range(ITERS):
        wait_all(allspend.at[it], send_sem.at[4 + it])


def deal(result, lam_out, mu_out, spend_out):
    tiles = lam_out.shape[1] // LANES
    for k in range(tiles):
        at = slice(k * LANES, (k + 1) * LANES)
        lam_out[:, at] = result[k : k + 1]
        spend_out[:, at] = result[tiles + k : tiles + k + 1]
    mu_out[...] = result[SUBLANES:]


def body(
    n,
    n_dev,
    values,
    costs,
    block_ids,
    row_counts,
    adv_map,
    camp_limits,
    adv_limits,
    camp_duals,
    adv_duals,
):
    blocks, rows, width = values.shape
    owned = camp_duals.shape[0]
    total = owned * n
    num_adv = adv_duals.shape[0]
    groups = num_adv // LANES
    eta = owned // width / (4.0 * rows * blocks)
    eta_adv = num_adv * (owned // width) / (4.0 * rows * blocks * total)
    smem = pl.BlockSpec(memory_space=pltpu.SMEM)
    vmem = pl.BlockSpec(memory_space=pltpu.VMEM)
    hbm = pl.BlockSpec(memory_space=pl.ANY)
    result = pl.pallas_call(
        functools.partial(kernel, n, n_dev, eta, eta_adv),
        out_shape=jax.ShapeDtypeStruct((SUBLANES + groups, LANES), jnp.float32),
        in_specs=[smem, smem, hbm, hbm] + [vmem] * 6,
        out_specs=vmem,
        scratch_shapes=[
            pltpu.VMEM((blocks, rows, width), jnp.bfloat16),
            pltpu.VMEM((blocks, rows, width), jnp.bfloat16),
            pltpu.VMEM((ITERS, n, 1, width), jnp.float32),
            pltpu.VMEM((4, total), jnp.float32),
            pltpu.VMEM((LANES, total), jnp.bfloat16),
            pltpu.VMEM((groups, total), jnp.float32),
            pltpu.VMEM((SLAB + 1, SLAB, LANES), jnp.float32),
            pltpu.VMEM((blocks * SUBLANES, width), jnp.float32),
            pltpu.VMEM((total // width, 1, width), jnp.float32),
            pltpu.VMEM((ITERS, n - 1, 1, width), jnp.float32),
            pltpu.VMEM((ITERS, 1, total), jnp.float32),
            pltpu.SemaphoreType.DMA((2, CHUNKS)),
            pltpu.SemaphoreType.DMA((6,)),
            pltpu.SemaphoreType.DMA((6,)),
        ],
        compiler_params=pltpu.CompilerParams(
            collective_id=0, has_side_effects=True, vmem_limit_bytes=56 * 1024 * 1024
        ),
        cost_estimate=pl.CostEstimate(
            flops=ITERS * 8 * blocks * rows * width,
            bytes_accessed=4 * blocks * rows * width,
            transcendentals=0,
        ),
    )(
        block_ids,
        row_counts,
        values,
        costs,
        block_ids.reshape(1, blocks),
        adv_map.reshape(1, owned),
        camp_limits.reshape(1, owned),
        adv_limits.reshape(groups, LANES),
        camp_duals.reshape(1, owned),
        adv_duals.reshape(groups, LANES),
    )
    lam, mu, spend = pl.pallas_call(
        deal,
        out_shape=(
            jax.ShapeDtypeStruct((1, owned), jnp.float32),
            jax.ShapeDtypeStruct((groups, LANES), jnp.float32),
            jax.ShapeDtypeStruct((1, owned), jnp.float32),
        ),
        in_specs=[vmem],
        out_specs=(vmem, vmem, vmem),
    )(result)
    return lam.reshape(owned), mu.reshape(num_adv), spend.reshape(owned)


def solution(mesh):
    both = P(("imp", "dev"))
    blocked = P(("imp", "dev"), None, None)
    return jax.shard_map(
        functools.partial(body, mesh.size, mesh.shape["dev"]),
        mesh=mesh,
        in_specs=(blocked, blocked, both, both, both, both, P(), both, P()),
        out_specs=(both, P(), both),
        check_vma=False,
    )
```

```python
import functools

import jax
import jax.numpy as jnp
from jax import lax
from jax.experimental import pallas as pl
from jax.experimental.pallas import tpu as pltpu
from jax.sharding import PartitionSpec as P

ITERS = 2
LANES = 128
SLAB = 16
SUBLANES = 8
CHUNKS = 4
MESH = pl.DeviceIdType.MESH


def split3(x):
    one = x.astype(jnp.bfloat16)
    rest = x - one.astype(jnp.float32)
    two = rest.astype(jnp.bfloat16)
    three = (rest - two.astype(jnp.float32)).astype(jnp.bfloat16)
    return jnp.concatenate([one, two, three], axis=0)


def split2(x):
    one = x.astype(jnp.bfloat16)
    return jnp.concatenate([one, (x - one.astype(jnp.float32)).astype(jnp.bfloat16)], axis=0)


def sum3(x):
    m = x.shape[0] // 3
    return x[:m] + x[m : 2 * m] + x[2 * m :]


def low_onehot(adv):
    width = adv.shape[1]
    rows = lax.broadcasted_iota(jnp.int32, (LANES, width), 0)
    hit = rows == jnp.bitwise_and(adv, LANES - 1)
    return jnp.where(hit, 1.0, 0.0).astype(jnp.bfloat16)


def high_onehot(adv, groups):
    width = adv.shape[1]
    rows = lax.broadcasted_iota(jnp.int32, (groups, width), 0)
    return jnp.where(rows == lax.shift_right_logical(adv, 7), 1.0, 0.0)


def take(mu3, low, high):
    picked = jnp.dot(mu3, low, preferred_element_type=jnp.float32)
    return jnp.sum(sum3(picked) * high, axis=0, keepdims=True)


def kernel(
    n,
    n_dev,
    eta,
    eta_adv,
    ids_s,
    counts_s,
    values,
    costs,
    ids_v,
    adv_ref,
    lim_ref,
    adv_lim_ref,
    lam_ref,
    mu_ref,
    result,
    vbuf,
    cbuf,
    price,
    static,
    low,
    high,
    vwide,
    cwide,
    cap,
    contrib,
    part,
    got,
    allspend,
    load_sem,
    send_sem,
    recv_sem,
):
    blocks, rows, width = vbuf.shape
    groups = mu_ref.shape[0]
    me = lax.axis_index("imp") * n_dev + lax.axis_index("dev")
    step_blocks = blocks // CHUNKS

    def load(i):
        where = pl.ds(i * step_blocks, step_blocks)
        return (
            pltpu.make_async_copy(values.at[where], vbuf.at[where], load_sem.at[0, i]),
            pltpu.make_async_copy(costs.at[where], cbuf.at[where], load_sem.at[1, i]),
        )

    for i in range(CHUNKS):
        for copy in load(i):
            copy.start()

    barrier = pltpu.get_barrier_semaphore()

    def peer(d):
        return lax.rem(me + d, n)

    def place(k):
        return (k // n_dev, lax.rem(k, n_dev))

    @pl.loop(1, n, unroll=True)
    def _(d):
        pl.semaphore_signal(barrier, inc=1, device_id=place(peer(d)), device_id_type=MESH)

    def lanes(k):
        return pl.ds(pl.multiple_of(k * width, width), width)

    def share(ref, phase):
        spot = ref.at[me] if len(ref.shape) == 3 else ref.at[:, lanes(me)]

        @pl.loop(1, n, unroll=True)
        def _(d):
            pltpu.make_async_remote_copy(
                src_ref=spot,
                dst_ref=spot,
                send_sem=send_sem.at[phase],
                recv_sem=recv_sem.at[phase],
                device_id=place(peer(d)),
                device_id_type=MESH,
            ).start()

    def wait_all(ref, sem):
        if len(ref.shape) == 3:
            span = ref.at[pl.ds(0, n - 1)]
        else:
            span = ref.at[:, pl.ds(0, (n - 1) * width)]
        pltpu.make_async_copy(span, span, sem).wait()

    def scatter(phase):
        @pl.loop(1, n, unroll=True)
        def _(d):
            to = peer(d)
            pltpu.make_async_remote_copy(
                src_ref=part.at[to],
                dst_ref=got.at[phase, d - 1],
                send_sem=send_sem.at[2 + phase],
                recv_sem=recv_sem.at[2 + phase],
                device_id=place(to),
                device_id_type=MESH,
            ).start()

    def wait_scatter(sem, phase):
        span = got.at[phase]
        pltpu.make_async_copy(span, span, sem).wait()

    adv = adv_ref[...]
    lam = lam_ref[...]
    mu = mu_ref[...]
    price[0, me] = lam + take(split3(mu), low_onehot(adv), high_onehot(adv, groups))
    static[:, lanes(me)] = jnp.concatenate(
        [lam, adv.astype(jnp.float32), lim_ref[...], jnp.zeros_like(lam)], axis=0
    )
    live_rows = lax.broadcasted_iota(jnp.int32, (SLAB, LANES), 0)
    for k in range(SLAB + 1):
        cap[k] = jnp.where(live_rows < k, 0.5, 0.0)

    pl.semaphore_wait(barrier, n - 1)
    share(price.at[0], 0)
    wait_all(price.at[0], recv_sem.at[0])
    share(static, 1)

    campaign = lax.broadcasted_iota(jnp.int32, (part.shape[0], blocks), 0)
    owner = jnp.where(campaign == ids_v[...], 1.0, 0.0).astype(jnp.bfloat16)
    wide = lax.broadcasted_iota(jnp.int32, (blocks, blocks * SUBLANES), 1)
    from_block = lax.broadcasted_iota(jnp.int32, (blocks, blocks * SUBLANES), 0)
    spread = jnp.where(lax.shift_right_logical(wide, 3) == from_block, 1.0, 0.0)
    owner = jnp.dot(
        owner, spread.astype(jnp.bfloat16), preferred_element_type=jnp.float32
    ).astype(jnp.bfloat16)
    owner2 = jnp.concatenate([owner, owner], axis=1)

    def block_pass(b, it, vfrom, cfrom):
        row = price[it, ids_s[b]]
        prices = [
            jnp.broadcast_to(row[:, h : h + LANES], (SLAB, LANES))
            for h in range(0, width, LANES)
        ]
        totals = [jnp.zeros((SLAB, LANES), jnp.float32) for _ in prices]
        count = counts_s[b]
        for s in range(0, rows, SLAB):
            top = cap[jnp.minimum(jnp.maximum(count - s, 0), SLAB)]
            for h, p in enumerate(prices):
                at = pl.ds(h * LANES, LANES)
                v = vfrom[b, pl.ds(s, SLAB), at].astype(jnp.float32)
                c = cfrom[b, pl.ds(s, SLAB), at].astype(jnp.float32)
                x = jnp.minimum(jnp.maximum(v - c * p, 0.0), top)
                totals[h] = totals[h] + c * x
        for h, total in enumerate(totals):
            where = pl.ds(pl.multiple_of(b * SUBLANES, SUBLANES), SUBLANES)
            contrib[where, pl.ds(h * LANES, LANES)] = 2.0 * (
                total[:SUBLANES] + total[SUBLANES:]
            )

    for it in range(ITERS):
        for i in range(CHUNKS):
            if it == 0:
                for copy in load(i):
                    copy.wait()
            span = step_blocks
            wide_now = it > 0 and i == 0
            vfrom, cfrom = (vwide, cwide) if wide_now else (vbuf, cbuf)

            @pl.loop(i * span, (i + 1) * span, unroll=4)
            def _(b):
                block_pass(b, it, vfrom, cfrom)

        mine = jnp.dot(owner2, split2(contrib[...]), preferred_element_type=jnp.float32)
        if it > 0:
            wait_scatter(send_sem.at[2 + it - 1], it - 1)
        for k in range(part.shape[0]):
            part[k] = mine[k : k + 1]
        scatter(it)
        if it == 0:
            wait_all(static, recv_sem.at[1])
            for k in range(n):
                every = static[1:2, pl.ds(k * width, width)].astype(jnp.int32)
                low[:, pl.ds(k * width, width)] = low_onehot(every)
                high[:, pl.ds(k * width, width)] = high_onehot(every, groups)
        wait_scatter(recv_sem.at[2 + it], it)
        spend = part[me] + jnp.sum(got[it], axis=0)
        allspend[it, :, lanes(me)] = spend
        share(allspend.at[it], 4 + it)
        lam = jnp.maximum(0.0, lam + eta * (spend - lim_ref[...]))
        if it == 0:

            @pl.loop(0, blocks // CHUNKS)
            def _(b):
                vwide[b] = vbuf[b].astype(jnp.float32)
                cwide[b] = cbuf[b].astype(jnp.float32)

        wait_all(allspend.at[it], recv_sem.at[4 + it])

        adv_spend = jnp.zeros((3 * groups, LANES), jnp.float32)
        stretch = min(n, 32) * width
        for first in range(0, n * width, stretch):
            at = pl.ds(first, stretch)
            adv_spend = adv_spend + lax.dot_general(
                split3(high[:, at] * allspend[it, :, at]),
                low[:, at],
                (((1,), (1,)), ((), ())),
                preferred_element_type=jnp.float32,
            )
        mu = jnp.maximum(0.0, mu + eta_adv * (sum3(adv_spend) - adv_lim_ref[...]))
        if it < ITERS - 1:
            mu3 = split3(mu)
            for first in range(0, n * width, stretch):
                at = pl.ds(first, stretch)
                lam_all = jnp.maximum(
                    0.0, static[0:1, at] + eta * (allspend[it, :, at] - static[2:3, at])
                )
                new = lam_all + take(mu3, low[:, at], high[:, at])
                for k in range(stretch // width):
                    price[it + 1, first // width + k] = new[:, k * width : (k + 1) * width]
    tiles = width // LANES
    for k in range(tiles):
        at = slice(k * LANES, (k + 1) * LANES)
        result[k : k + 1] = lam[:, at]
        result[tiles + k : tiles + k + 1] = spend[:, at]
    result[SUBLANES:] = mu
    wait_all(price.at[0], send_sem.at[0])
    wait_all(static, send_sem.at[1])
    wait_scatter(send_sem.at[2 + ITERS - 1], ITERS - 1)
    for it in range(ITERS):
        wait_all(allspend.at[it], send_sem.at[4 + it])


def deal(result, lam_out, mu_out, spend_out):
    tiles = lam_out.shape[1] // LANES
    for k in range(tiles):
        at = slice(k * LANES, (k + 1) * LANES)
        lam_out[:, at] = result[k : k + 1]
        spend_out[:, at] = result[tiles + k : tiles + k + 1]
    mu_out[...] = result[SUBLANES:]


def body(
    n,
    n_dev,
    values,
    costs,
    block_ids,
    row_counts,
    adv_map,
    camp_limits,
    adv_limits,
    camp_duals,
    adv_duals,
):
    blocks, rows, width = values.shape
    owned = camp_duals.shape[0]
    total = owned * n
    num_adv = adv_duals.shape[0]
    groups = num_adv // LANES
    eta = owned // width / (4.0 * rows * blocks)
    eta_adv = num_adv * (owned // width) / (4.0 * rows * blocks * total)
    smem = pl.BlockSpec(memory_space=pltpu.SMEM)
    vmem = pl.BlockSpec(memory_space=pltpu.VMEM)
    hbm = pl.BlockSpec(memory_space=pl.ANY)
    result = pl.pallas_call(
        functools.partial(kernel, n, n_dev, eta, eta_adv),
        out_shape=jax.ShapeDtypeStruct((SUBLANES + groups, LANES), jnp.float32),
        in_specs=[smem, smem, hbm, hbm] + [vmem] * 6,
        out_specs=vmem,
        scratch_shapes=[
            pltpu.VMEM((blocks, rows, width), jnp.bfloat16),
            pltpu.VMEM((blocks, rows, width), jnp.bfloat16),
            pltpu.VMEM((ITERS, n, 1, width), jnp.float32),
            pltpu.VMEM((4, total), jnp.float32),
            pltpu.VMEM((LANES, total), jnp.bfloat16),
            pltpu.VMEM((groups, total), jnp.float32),
            pltpu.VMEM((blocks // CHUNKS, rows, width), jnp.float32),
            pltpu.VMEM((blocks // CHUNKS, rows, width), jnp.float32),
            pltpu.VMEM((SLAB + 1, SLAB, LANES), jnp.float32),
            pltpu.VMEM((blocks * SUBLANES, width), jnp.float32),
            pltpu.VMEM((total // width, 1, width), jnp.float32),
            pltpu.VMEM((ITERS, n - 1, 1, width), jnp.float32),
            pltpu.VMEM((ITERS, 1, total), jnp.float32),
            pltpu.SemaphoreType.DMA((2, CHUNKS)),
            pltpu.SemaphoreType.DMA((6,)),
            pltpu.SemaphoreType.DMA((6,)),
        ],
        compiler_params=pltpu.CompilerParams(
            collective_id=0, has_side_effects=True, vmem_limit_bytes=56 * 1024 * 1024
        ),
        cost_estimate=pl.CostEstimate(
            flops=ITERS * 8 * blocks * rows * width,
            bytes_accessed=4 * blocks * rows * width,
            transcendentals=0,
        ),
    )(
        block_ids,
        row_counts,
        values,
        costs,
        block_ids.reshape(1, blocks),
        adv_map.reshape(1, owned),
        camp_limits.reshape(1, owned),
        adv_limits.reshape(groups, LANES),
        camp_duals.reshape(1, owned),
        adv_duals.reshape(groups, LANES),
    )
    lam, mu, spend = pl.pallas_call(
        deal,
        out_shape=(
            jax.ShapeDtypeStruct((1, owned), jnp.float32),
            jax.ShapeDtypeStruct((groups, LANES), jnp.float32),
            jax.ShapeDtypeStruct((1, owned), jnp.float32),
        ),
        in_specs=[vmem],
        out_specs=(vmem, vmem, vmem),
    )(result)
    return lam.reshape(owned), mu.reshape(num_adv), spend.reshape(owned)


def solution(mesh):
    both = P(("imp", "dev"))
    blocked = P(("imp", "dev"), None, None)
    return jax.shard_map(
        functools.partial(body, mesh.size, mesh.shape["dev"]),
        mesh=mesh,
        in_specs=(blocked, blocked, both, both, both, both, P(), both, P()),
        out_specs=(both, P(), both),
        check_vma=False,
    )
```
